128 devices in a mesh: dp: 2 (over z_lo), ctx: 16 (over z_hi, y, core), tensor: 4 (over x).
Axes of the slice: x: 4, y: 4, z: 4 (z_hi: 2, z_lo: 2; z = z_hi * 2 + z_lo), core: 2. Of those that a mesh axis runs over, the one named last changes fastest.
Arguments:
- normed_input: bfloat16 [2, 8192, 9216], P('dp', ('ctx', 'tensor')), may hold values from -16 to 16
- queries: bfloat16 [2, 8192, 3072], P('dp', 'ctx', 'tensor'), may hold values from -10 to 10
- key_heads: bfloat16 [2, 8192, 512], P('dp', 'ctx', 'tensor'), may hold values from -10 to 10
- value_heads: bfloat16 [2, 8192, 512], P('dp', 'ctx', 'tensor'), may hold values from -6 to 6
- attn_out: bfloat16 [2, 8192, 3072], P('dp', 'ctx', 'tensor'), may hold values from -6 to 6
- out_grad: bfloat16 [2, 8192, 3072], P('dp', 'ctx', 'tensor'), may hold values from -6 to 6
- key_weight: bfloat16 [9216, 512], P(None, 'tensor'), may hold values from -0.5 to 0.5
- value_weight: bfloat16 [9216, 512], P(None, 'tensor'), may hold values from -0.5 to 0.5
- block_order: int32 [32], replicated, may hold values from 0 to 31, each once
Outputs:
- query_grad: bfloat16 [2, 8192, 3072], P('dp', 'ctx', 'tensor')
- input_grad: bfloat16 [2, 8192, 9216], P('dp', ('ctx', 'tensor'))
- keyproj_grad: bfloat16 [9216, 512], P(('dp', 'ctx'), 'tensor')
- valueproj_grad: bfloat16 [9216, 512], P(('dp', 'ctx'), 'tensor')
The draws below stay inside these ranges and needn't reach their ends.
Inputs may be any that keep to these rules, and one draw needn't show every extreme that they name: Each block number appears once; stored block c of every sequence holds the places block_order[c] * 256 to block_order[c] * 256 + 255 in order.
All inputs are finite; a program needn't handle non-finite values.
Results may differ from the reference program's by a relative error of at most 0.014.
Values may be sent and summed in bfloat16 or wider, within the bound.
No kernel may reach another device: no remote copies, remote signals or barrier semaphores. Data moves between devices by JAX's collectives and lax.ppermute only.
A program may use at most 128 MiB of HBM per device.

```python
import jax
import jax.numpy as jnp
from jax import lax

D = 9216
HD = 128
HQ = 6
KV_DEV = 1
TOK_DEV = 128
BLOCK = 256
NBLK = 32
LENGTH = 8192
KV_HEADS = 4
SEQS = 2
N_TENSOR = 4


def draw_queries(key, part):
    key = jax.random.fold_in(key, 11)
    full_shape = (SEQS, LENGTH, KV_HEADS, HQ, HD)
    values = jnp.clip(jax.random.normal(key, full_shape, jnp.float32), -6.0, 6.0)
    return values.reshape(SEQS, LENGTH, KV_HEADS * HQ * HD).astype(jnp.bfloat16)


def draw_key_heads(key, part):
    key = jax.random.fold_in(key, 12)
    full_shape = (SEQS, LENGTH, KV_HEADS, HD)
    values = jnp.clip(jax.random.normal(key, full_shape, jnp.float32), -6.0, 6.0)
    return values.reshape(SEQS, LENGTH, KV_HEADS * HD).astype(jnp.bfloat16)


def with_spikes(entries, key, source, target, parts, factor):
    def block_of(dim):
        return (jnp.arange(entries.shape[dim]) // (entries.shape[dim] // parts)).reshape((-1,) + (1,) * (entries.ndim - 1 - dim))

    first = jax.random.permutation(key, parts)[block_of(target)]
    other_side = (block_of(target) + parts // 2) % parts
    return jnp.where((block_of(source) == first) | (block_of(source) == other_side), factor * entries, entries)


def steps_of(key, dims, pieces, least, high):
    factor_of = 1.0
    for position, blocks in pieces:
        steps = jax.random.uniform(jax.random.fold_in(jax.random.fold_in(key, 6), position), (blocks,), jnp.float32, least / len(pieces), high / len(pieces))
        factor_of = factor_of * jnp.repeat(jnp.exp(steps), dims[position] // blocks).reshape((-1,) + (1,) * (len(dims) - 1 - position))
    return factor_of


def bell_draw(stream_key, shape, spread, limit, split=(), held_as=jnp.bfloat16):
    level = steps_of(stream_key, shape, split, -0.22, 0.18) if split else 1.0
    result = jax.random.normal(stream_key, shape, jnp.float32) * spread * level
    return jnp.minimum(jnp.maximum(result, -limit), limit).astype(held_as)


def noise_with(rng, extent, scale, reach, shards, heavy, kind=jnp.bfloat16):
    values = scale * jax.random.normal(rng, extent, jnp.float32)
    if shards:
        values = values * steps_of(rng, extent, shards, -0.22, 0.18)
    return jnp.clip(with_spikes(values, jax.random.fold_in(rng, 3), *heavy), -reach, reach).astype(kind)


def setup_inputs(seed: int = 0) -> dict:
    key_list = jax.random.split(jax.random.key(seed), 10)
    normed_input = noise_with(key_list[0], (SEQS, LENGTH, D), 1.0, 16.0, ((0, 2), (1, 64)), (1, 2, 64, 4.0))
    queries = draw_queries(jax.random.fold_in(key_list[9], 71), 0)
    key_heads = draw_key_heads(jax.random.fold_in(key_list[9], 71), 0)
    value_heads = bell_draw(key_list[3], (SEQS, LENGTH, KV_HEADS * HD), 1.0, 6.0, ((0, 2), (1, 16), (2, 4)))
    attn_out = bell_draw(key_list[4], (SEQS, LENGTH, KV_HEADS * HQ * HD), 1.0, 6.0, ((0, 2), (1, 16), (2, 4)))
    out_grad = bell_draw(key_list[5], (SEQS, LENGTH, KV_HEADS * HQ * HD), 1.0, 6.0, ((0, 2), (1, 16), (2, 4)))
    key_weight = bell_draw(key_list[6], (D, KV_HEADS * HD), HD ** -0.5, 0.5, ((1, 4),))
    value_weight = bell_draw(key_list[7], (D, KV_HEADS * HD), HD ** -0.5, 0.5, ((1, 4),))
    block_order = jax.random.permutation(key_list[8], NBLK).astype(jnp.int32)
    return dict(normed_input=normed_input, queries=queries, key_heads=key_heads, value_heads=value_heads, attn_out=attn_out, out_grad=out_grad, key_weight=key_weight, value_weight=value_weight, block_order=block_order)


NEG_BIG = -1e30


def sequence_places(block_order):
    row_ids = jnp.arange(LENGTH, dtype=jnp.int32)
    return (block_order[row_ids // BLOCK] * BLOCK + row_ids % BLOCK).astype(jnp.int32)


def group_grads(query_rows, key_rows, value_rows, out_rows, grad_rows, places):
    span_rows = TOK_DEV * N_TENSOR
    count_blocks = LENGTH // span_rows
    score_scale = HD ** -0.5
    key_full = key_rows.astype(jnp.float32)
    value_full = value_rows.astype(jnp.float32)

    def one_block(running, block_pack):
        key_acc, value_acc = running
        query_part, out_part, grad_part, query_places = block_pack
        query_full = query_part.astype(jnp.float32)
        grad_full = grad_part.astype(jnp.float32)
        raw_scores = jnp.einsum("rhd,nd->hrn", query_full, key_full) * score_scale
        allowed = (places[None, :] <= query_places[:, None])[None]
        row_top = jnp.max(jnp.where(allowed, raw_scores, NEG_BIG), axis=-1)
        row_total = jnp.sum(jnp.where(allowed, jnp.exp(raw_scores - row_top[..., None]), 0.0), axis=-1)
        log_total = row_top + jnp.log(row_total)
        attn_probs = jnp.where(allowed, jnp.exp(raw_scores - log_total[..., None]), 0.0)
        out_dot = jnp.sum(grad_full * out_part.astype(jnp.float32), axis=-1).T
        grad_probs = jnp.einsum("rhd,nd->hrn", grad_full, value_full)
        grad_scores = lax.optimization_barrier((attn_probs * (grad_probs - out_dot[..., None])).astype(jnp.bfloat16)).astype(jnp.float32)
        probs_half = lax.optimization_barrier(attn_probs.astype(jnp.bfloat16)).astype(jnp.float32)
        query_grad = jnp.einsum("hrn,nd->rhd", grad_scores, key_full) * score_scale
        key_acc = key_acc + jnp.einsum("hrn,rhd->nd", grad_scores, query_full) * score_scale
        value_acc = value_acc + jnp.einsum("hrn,rhd->nd", probs_half, grad_full)
        return (key_acc, value_acc), query_grad

    initial = (jnp.zeros((LENGTH, HD), jnp.float32), jnp.zeros((LENGTH, HD), jnp.float32))
    packs = (query_rows.reshape(count_blocks, span_rows, HQ, HD),
             out_rows.reshape(count_blocks, span_rows, HQ, HD),
             grad_rows.reshape(count_blocks, span_rows, HQ, HD),
             places.reshape(count_blocks, span_rows))
    (key_acc, value_acc), query_blocks = lax.scan(one_block, initial, packs)
    return query_blocks.reshape(LENGTH, HQ, HD), key_acc, value_acc


def reference(normed_input, queries, key_heads, value_heads, attn_out, out_grad, key_weight, value_weight, block_order):
    places = sequence_places(block_order)
    query_list = []
    input_list = []
    key_total = jnp.zeros((D, KV_HEADS * HD), jnp.float32)
    value_total = jnp.zeros((D, KV_HEADS * HD), jnp.float32)
    for seq_index in range(SEQS):
        query_view = queries[seq_index].reshape(LENGTH, KV_HEADS, HQ, HD)
        out_view = attn_out[seq_index].reshape(LENGTH, KV_HEADS, HQ, HD)
        grad_view = out_grad[seq_index].reshape(LENGTH, KV_HEADS, HQ, HD)
        key_view = key_heads[seq_index].reshape(LENGTH, KV_HEADS, HD)
        value_view = value_heads[seq_index].reshape(LENGTH, KV_HEADS, HD)
        query_cols = []
        key_cols = []
        value_cols = []
        for group in range(KV_HEADS):
            group_query, group_key, group_value = group_grads(query_view[:, group], key_view[:, group], value_view[:, group], out_view[:, group], grad_view[:, group], places)
            query_cols.append(group_query)
            key_cols.append(group_key)
            value_cols.append(group_value)
        query_list.append(jnp.stack(query_cols, axis=1).reshape(LENGTH, KV_HEADS * HQ * HD))
        key_half = jnp.stack(key_cols, axis=1).reshape(LENGTH, KV_HEADS * HD).astype(jnp.bfloat16)
        value_half = jnp.stack(value_cols, axis=1).reshape(LENGTH, KV_HEADS * HD).astype(jnp.bfloat16)
        summed = jnp.zeros((LENGTH, D), jnp.float32)
        for tensor_index in range(N_TENSOR):
            low = tensor_index * KV_DEV * HD
            high = low + KV_DEV * HD
            tensor_part = jnp.dot(key_half[:, low:high], key_weight[:, low:high].T, preferred_element_type=jnp.float32)
            tensor_part = tensor_part + jnp.dot(value_half[:, low:high], value_weight[:, low:high].T, preferred_element_type=jnp.float32)
            summed = summed + lax.optimization_barrier(tensor_part.astype(jnp.bfloat16)).astype(jnp.float32)
        input_list.append(summed.astype(jnp.bfloat16))
        key_total = key_total + jnp.dot(normed_input[seq_index].T, key_half, preferred_element_type=jnp.float32)
        value_total = value_total + jnp.dot(normed_input[seq_index].T, value_half, preferred_element_type=jnp.float32)
    query_grad = jnp.stack(query_list).astype(jnp.bfloat16)
    input_grad = jnp.stack(input_list)
    return (query_grad, input_grad, key_total.astype(jnp.bfloat16), value_total.astype(jnp.bfloat16))
```

```python
import functools

import jax
import jax.numpy as jnp
from jax import lax
from jax.experimental import pallas as pl
from jax.experimental.pallas import tpu as pltpu
from jax.sharding import PartitionSpec as P

HD = 128
HQ = 6
NH = 3
BLK = 256
NX = 4
LOG2E = 1.4426950408889634
NEG = -1e30
SC = HD ** (-0.5)
F32 = jnp.float32
BF = jnp.bfloat16

CORE_PERM = [(i, i ^ 1) for i in range(16)]
ZHI_PERM = [(i, i ^ 8) for i in range(16)]
CHIP_GROUPS = [[2 * i + c for i in range(8)] for c in range(2)]
ALL_CHIP_GROUPS = [[2 * i + c for i in range(16)] for c in range(2)]


def y_perm(by):
    return [(i, (i & 9) | (((((i >> 1) & 3) + by) & 3) << 1)) for i in range(16)]


def x_perm(by):
    return [(i, (i + by) % NX) for i in range(NX)]


def cx_perm(flip, by):
    return [(i, (((i >> 2) ^ flip) << 2) | ((i + by) & 3)) for i in range(64)]


def home_perm():
    pairs = []
    for i in range(128):
        dp, ctx, t = i >> 6, (i >> 2) & 15, i & 3
        core, piece = ctx & 1, dp * 8 + (ctx >> 1)
        row, dx = core * 16 + t * 4 + (piece >> 2), piece & 3
        pairs.append((i, row * 4 + ((t + dx) & 3)))
    return pairs


def load_pair(own, got, dst, core, sem, at):
    half = own.shape[0]
    cols = pl.ds(pl.multiple_of(core * (NH * HD), HD), NH * HD)
    copies = [
        pltpu.make_async_copy(own.at[:, cols], dst.at[0:half, :], sem.at[at]),
        pltpu.make_async_copy(got, dst.at[half : 2 * half, :], sem.at[at + 1]),
    ]
    for c in copies:
        c.start()
    return copies


def load_slots(refs, dst, cols, sem, at):
    copies = []
    row = 0
    for n, ref in enumerate(refs):
        r = pl.ds(row, ref.shape[0])
        copies.append(pltpu.make_async_copy(ref, dst.at[r, cols], sem.at[at + n]))
        copies[-1].start()
        row += ref.shape[0]
    return copies


def put_scores_side(qT, b, cw, q):
    scaled = q.astype(F32) * (SC * LOG2E)
    hi = scaled.astype(BF)
    lo = (scaled - hi.astype(F32)).astype(BF)
    qT[b, 0:HD, cw] = hi.T
    qT[b, HD : 2 * HD, cw] = lo.T


def scores(kaug, qT, b, kp):
    r = pl.ds(pl.multiple_of(kp * BLK, BLK), BLK)
    return jnp.dot(kaug[r, :], qT[b], preferred_element_type=F32)


def causal():
    key_i = lax.broadcasted_iota(jnp.int32, (BLK, NH * BLK), 0)
    qry_i = lax.broadcasted_iota(jnp.int32, (BLK, NH * BLK), 1) % BLK
    return key_i <= qry_i


def over_keys(rank, pos_ref, step, width):
    def one(j, _):
        step(j, False)
        return 0

    def wide(j, _):
        for u in range(width):
            step(width * j + u, False)
        return 0

    lax.fori_loop(0, rank // width, wide, 0)
    lax.fori_loop(width * (rank // width), rank, one, 0)
    step(rank, True)


def stats_kernel(rank_ref, pos_ref, core_ref, q_own, q_got, *rest, nq, n_slots):
    k_refs = rest[:n_slots]
    lse = rest[n_slots]
    qs, kaug, qT, m_s, l_s, sem, sem_k = rest[n_slots + 1 :]
    W = NH * BLK
    first = load_pair(q_own, q_got, qs, core_ref[0], sem, 0)
    copies = load_slots(k_refs, kaug, pl.ds(0, HD), sem_k, 0)
    copies += load_slots(k_refs, kaug, pl.ds(HD, HD), sem_k, n_slots)
    for c in first:
        c.wait()

    def prep(b, _):
        r = pl.ds(pl.multiple_of(b * BLK, BLK), BLK)
        for h in range(NH):
            put_scores_side(qT, b, pl.ds(h * BLK, BLK), qs[r, pl.ds(h * HD, HD)])
        return 0

    lax.fori_loop(0, nq, prep, 0)
    for c in copies:
        c.wait()
    allowed = causal()

    def q_loop(b, _):
        def step(j, diag):
            s = scores(kaug, qT, b, pos_ref[j])
            if diag:
                s = jnp.where(allowed, s, NEG)
            s3 = s.reshape(BLK // 8, 8, W)
            m0 = m_s[...]
            m1 = jnp.maximum(m0, jnp.max(s3, axis=0))
            l_s[...] = l_s[...] * jnp.exp2(m0 - m1) + jnp.sum(jnp.exp2(s3 - m1[None]), axis=0)
            m_s[...] = m1

        m_s[...] = jnp.full((8, W), NEG, F32)
        l_s[...] = jnp.zeros((8, W), F32)
        over_keys(rank_ref[b], pos_ref, step, 2)
        m = m_s[...]
        top = jnp.max(m, axis=0, keepdims=True)
        total = jnp.sum(l_s[...] * jnp.exp2(m - top), axis=0, keepdims=True)
        lse[b] = top + jnp.log2(total)
        return 0

    lax.fori_loop(0, nq, q_loop, 0)


def grads_kernel(
    rank_ref, pos_ref, to_ref, core_ref, lse, q_own, q_got, do_own, o_own, do_o_got, *rest, nq, n_slots
):
    k_refs = rest[:n_slots]
    v_refs = rest[n_slots : 2 * n_slots]
    dq_keep, dq_send, dkv0, dkv1 = rest[2 * n_slots : 2 * n_slots + 4]
    qs, dos, os, kaug, vaug, qT, doT, qn, don, dqT, dkv, sem, sem_kv = rest[2 * n_slots + 4 :]
    W = NH * BLK
    half = nq * BLK // 2
    nblk = kaug.shape[0] // BLK
    core = core_ref[0]
    first = load_pair(q_own, q_got, qs, core, sem, 0)
    first += load_pair(do_own, do_o_got.at[0], dos, core, sem, 2)
    first += load_pair(o_own, do_o_got.at[1], os, core, sem, 4)
    copies = load_slots(k_refs, kaug, pl.ds(0, HD), sem_kv, 0)
    copies += load_slots(k_refs, kaug, pl.ds(HD, HD), sem_kv, n_slots)
    copies += load_slots(v_refs, vaug, pl.ds(0, HD), sem_kv, 2 * n_slots)
    lane = lax.broadcasted_iota(jnp.int32, (BLK, HD), 1)
    ones = jnp.where(lane < 3, 1.0, 0.0).astype(BF)

    def init(i, _):
        r = pl.ds(pl.multiple_of(i * BLK, BLK), BLK)
        vaug[r, HD : 2 * HD] = ones
        dkv[r, :] = jnp.zeros((BLK, 2 * HD), F32)
        return 0

    lax.fori_loop(0, nblk, init, 0)
    for c in first:
        c.wait()

    def prep(b, _):
        r = pl.ds(pl.multiple_of(b * BLK, BLK), BLK)
        for h in range(NH):
            cq = pl.ds(h * HD, HD)
            cw = pl.ds(h * BLK, BLK)
            q = qs[r, cq]
            do = dos[r, cq]
            o = os[r, cq]
            qn[b, cw, :] = q
            don[b, cw, :] = do
            put_scores_side(qT, b, cw, q)
            doT[b, 0:HD, cw] = do.T
            d = -jnp.sum((do.astype(F32) * o.astype(F32)).T, axis=0, keepdims=True)
            d1 = d.astype(BF).astype(F32)
            d2 = (d - d1).astype(BF).astype(F32)
            d3 = d - d1 - d2
            sub = lax.broadcasted_iota(jnp.int32, (HD, BLK), 0)
            aug = jnp.where(sub == 0, d1, jnp.where(sub == 1, d2, jnp.where(sub == 2, d3, 0.0)))
            doT[b, HD : 2 * HD, cw] = aug.astype(BF)
        return 0

    lax.fori_loop(0, nq, prep, 0)
    for c in copies:
        c.wait()
    allowed = causal()

    def q_loop(b, _):
        def step(j, diag):
            kp = pos_ref[j]
            r = pl.ds(pl.multiple_of(kp * BLK, BLK), BLK)
            to = pl.ds(pl.multiple_of(to_ref[j] * BLK, BLK), BLK)
            p = jnp.exp2(scores(kaug, qT, b, kp) - lse[b])
            if diag:
                p = jnp.where(allowed, p, 0.0)
            dp = jnp.dot(vaug[r, :], doT[b], preferred_element_type=F32)
            p16 = p.astype(BF)
            ds16 = (p * dp).astype(BF)
            dkv[to, HD : 2 * HD] += jnp.dot(p16, don[b], preferred_element_type=F32)
            dkv[to, 0:HD] += jnp.dot(ds16, qn[b], preferred_element_type=F32)
            dqT[...] += lax.dot_general(
                kaug[r, 0:HD], ds16, (((0,), (0,)), ((), ())), preferred_element_type=F32
            )

        dqT[...] = jnp.zeros(dqT.shape, F32)
        over_keys(rank_ref[b], pos_ref, step, 2)
        for h in range(NH):
            qs[pl.ds(pl.multiple_of(b * BLK, BLK), BLK), pl.ds(h * HD, HD)] = (
                dqT[:, pl.ds(h * BLK, BLK)].T * SC
            ).astype(BF)
        return 0

    lax.fori_loop(0, nq, q_loop, 0)
    dq_keep[...] = qs[0:half, :]
    dq_send[...] = qs[half : 2 * half, :]

    def finish(i, _):
        r = pl.ds(pl.multiple_of(i * BLK, BLK), BLK)
        r1 = pl.ds(pl.multiple_of((i + nblk // 2) * BLK, BLK), BLK)
        dkv0[r, 0:HD] = (dkv[r, 0:HD] * SC).astype(BF)
        dkv0[r, HD : 2 * HD] = dkv[r, HD : 2 * HD].astype(BF)
        dkv1[r, 0:HD] = (dkv[r1, 0:HD] * SC).astype(BF)
        dkv1[r, HD : 2 * HD] = dkv[r1, HD : 2 * HD].astype(BF)
        return 0

    lax.fori_loop(0, nblk // 2, finish, 0)


VM = pl.BlockSpec(memory_space=pltpu.VMEM)
SM = pl.BlockSpec(memory_space=pltpu.SMEM)
HB = pl.BlockSpec(memory_space=pl.ANY)


BIG = 60 * 1024 * 1024


def softmax_stats(rank, pos, core, q, q_got, k_slots):
    half = q.shape[0]
    nq = 2 * half // BLK
    keys = sum(k.shape[0] for k in k_slots)
    W = NH * BLK
    n = len(k_slots)
    pairs = 66 * W * BLK
    return pl.pallas_call(
        functools.partial(stats_kernel, nq=nq, n_slots=n),
        out_shape=jax.ShapeDtypeStruct((nq, 1, W), F32),
        in_specs=[SM] * 3 + [HB] * (2 + n),
        out_specs=VM,
        scratch_shapes=[
            pltpu.VMEM((2 * half, NH * HD), BF),
            pltpu.VMEM((keys, 2 * HD), BF),
            pltpu.VMEM((nq, 2 * HD, W), BF),
            pltpu.VMEM((8, W), F32),
            pltpu.VMEM((8, W), F32),
            pltpu.SemaphoreType.DMA((2,)),
            pltpu.SemaphoreType.DMA((2 * n,)),
        ],
        compiler_params=pltpu.CompilerParams(vmem_limit_bytes=BIG),
        cost_estimate=pl.CostEstimate(
            flops=16 * pairs * HD, bytes_accessed=4 * 1024 * 1024, transcendentals=pairs
        ),
        name="softmax_stats",
    )(rank, pos, core, q, q_got, *k_slots)


def attention_grads(rank, pos, to, core, lse, q, q_got, do, o, do_o_got, k_slots, v_slots):
    half = q.shape[0]
    nq = 2 * half // BLK
    keys = sum(k.shape[0] for k in k_slots)
    W = NH * BLK
    n = len(k_slots)
    pairs = 66 * W * BLK
    return pl.pallas_call(
        functools.partial(grads_kernel, nq=nq, n_slots=n),
        out_shape=(
            jax.ShapeDtypeStruct((half, NH * HD), BF),
            jax.ShapeDtypeStruct((half, NH * HD), BF),
            jax.ShapeDtypeStruct((keys // 2, 2 * HD), BF),
            jax.ShapeDtypeStruct((keys // 2, 2 * HD), BF),
        ),
        in_specs=[SM] * 4 + [VM] + [HB] * (5 + 2 * n),
        out_specs=(VM,) * 4,
        scratch_shapes=[
            pltpu.VMEM((2 * half, NH * HD), BF),
            pltpu.VMEM((2 * half, NH * HD), BF),
            pltpu.VMEM((2 * half, NH * HD), BF),
            pltpu.VMEM((keys, 2 * HD), BF),
            pltpu.VMEM((keys, 2 * HD), BF),
            pltpu.VMEM((nq, 2 * HD, W), BF),
            pltpu.VMEM((nq, 2 * HD, W), BF),
            pltpu.VMEM((nq, W, HD), BF),
            pltpu.VMEM((nq, W, HD), BF),
            pltpu.VMEM((HD, W), F32),
            pltpu.VMEM((keys, 2 * HD), F32),
            pltpu.SemaphoreType.DMA((6,)),
            pltpu.SemaphoreType.DMA((3 * n,)),
        ],
        compiler_params=pltpu.CompilerParams(vmem_limit_bytes=BIG),
        cost_estimate=pl.CostEstimate(
            flops=32 * pairs * HD, bytes_accessed=16 * 1024 * 1024, transcendentals=pairs
        ),
        name="attention_grads",
    )(rank, pos, to, core, lse, q, q_got, do, o, do_o_got, *k_slots, *v_slots)


def load_grads(here, g_refs, g_all, sem):
    copies = []
    for cs in range(2):
        for dx in range(NX):
            for d in range(NX):
                chunk = (here + d) % NX
                n = (cs * NX + dx) * NX + d
                src = g_refs[cs][dx].at[pl.ds(pl.multiple_of(chunk * HD, HD), HD), :]
                dst = g_all.at[pl.ds((cs * NX + d) * HD, HD), pl.ds(dx * 2 * HD, 2 * HD)]
                copies.append(pltpu.make_async_copy(src, dst, sem.at[n]))
    for c in copies:
        c.start()
    return copies


def input_kernel(here_ref, *rest):
    here = here_ref[0]
    g_refs = (rest[0:4], rest[4:8])
    w_refs = rest[8:12]
    outs = rest[12:20]
    g_all, w_all, sem, sem_w = rest[20:]
    copies = load_grads(here, g_refs, g_all, sem)
    for n in range(8):
        dst = w_all.at[:, pl.ds(n * HD, HD)]
        copies.append(pltpu.make_async_copy(w_refs[n // 2].at[n % 2], dst, sem_w.at[n]))
        copies[-1].start()
    for c in copies:
        c.wait()
    cols = w_all.shape[0]
    for at in range(0, cols, 2 * HD):
        c = pl.ds(at, min(2 * HD, cols - at))
        block = lax.dot_general(
            g_all[...], w_all[c, :], (((1,), (1,)), ((), ())), preferred_element_type=F32
        ).astype(BF)
        for n, out in enumerate(outs):
            out[:, c] = block[n * HD : (n + 1) * HD]


def input_blocks(here, g_slots, w_slots):
    cols = w_slots[0].shape[1]
    return pl.pallas_call(
        input_kernel,
        out_shape=tuple(jax.ShapeDtypeStruct((HD, cols), BF) for _ in range(8)),
        in_specs=[SM] + [HB] * 12,
        out_specs=(VM,) * 8,
        scratch_shapes=[
            pltpu.VMEM((8 * HD, 8 * HD), BF),
            pltpu.VMEM((cols, 8 * HD), BF),
            pltpu.SemaphoreType.DMA((32,)),
            pltpu.SemaphoreType.DMA((8,)),
        ],
        compiler_params=pltpu.CompilerParams(vmem_limit_bytes=BIG),
        cost_estimate=pl.CostEstimate(
            flops=2 * 1024 * 1024 * cols, bytes_accessed=7 * 1024 * 1024, transcendentals=0
        ),
        name="input_blocks",
    )(here, *g_slots[0], *g_slots[1], *w_slots)


def turn_kernel(*rest):
    x_refs, out = rest[:NX], rest[NX]
    for cs in range(2):
        for d in range(NX):
            n = cs * NX + d
            out[:, pl.ds(n * HD, HD)] = x_refs[(-d) % NX][cs].T


def turn_columns(x_slots):
    cols = x_slots[0].shape[2]
    return pl.pallas_call(
        turn_kernel,
        out_shape=jax.ShapeDtypeStruct((cols, 8 * HD), BF),
        in_specs=[VM] * NX,
        out_specs=VM,
        compiler_params=pltpu.CompilerParams(vmem_limit_bytes=BIG),
        name="turn_columns",
    )(*x_slots)


def proj_kernel(here_ref, *rest):
    here = here_ref[0]
    g_refs = (rest[0:4], rest[4:8])
    x_turned, out, g_all, sem = rest[8:]
    for c in load_grads(here, g_refs, g_all, sem):
        c.wait()
    part = x_turned.shape[0] // 4
    for dx in range(NX):
        block = jnp.dot(
            x_turned[...], g_all[:, pl.ds(dx * 2 * HD, 2 * HD)], preferred_element_type=F32
        ).astype(BF)
        for i in range(4):
            out[i * 4 + dx] = block[i * part : (i + 1) * part]


def proj_parts(here, g_slots, x_turned):
    cols = x_turned.shape[0]
    return pl.pallas_call(
        proj_kernel,
        out_shape=jax.ShapeDtypeStruct((16, cols // 4, 2 * HD), BF),
        in_specs=[SM] + [HB] * 8 + [VM],
        out_specs=VM,
        scratch_shapes=[
            pltpu.VMEM((8 * HD, 8 * HD), BF),
            pltpu.SemaphoreType.DMA((32,)),
        ],
        compiler_params=pltpu.CompilerParams(vmem_limit_bytes=BIG),
        cost_estimate=pl.CostEstimate(
            flops=2 * 1024 * 1024 * cols, bytes_accessed=7 * 1024 * 1024, transcendentals=0
        ),
        name="proj_parts",
    )(here, *g_slots[0], *g_slots[1], x_turned)


def place_kernel(where_ref, *rest):
    core, here = where_ref[0], where_ref[1]
    parts, out = rest[:8], rest[8]
    cols = parts[0].shape[1]
    for cs in range(2):
        for dx in range(NX):
            at = ((core + cs) % 2) * (NX * cols) + ((here - dx + NX) % NX) * cols
            out[:, pl.ds(pl.multiple_of(at, HD), cols)] = parts[cs * NX + dx][...]


def place(where, parts):
    rows, cols = parts[0].shape
    return pl.pallas_call(
        place_kernel,
        out_shape=jax.ShapeDtypeStruct((rows, 8 * cols), BF),
        in_specs=[SM] + [VM] * 8,
        out_specs=VM,
        compiler_params=pltpu.CompilerParams(vmem_limit_bytes=BIG),
        name="place_columns",
    )(where, *parts)


def summed(*terms):
    total = terms[0].astype(F32)
    for term in terms[1:]:
        total = total + term.astype(F32)
    return total


def per_device(
    normed_input,
    queries,
    key_heads,
    value_heads,
    attn_out,
    out_grad,
    key_weight,
    value_weight,
    block_order,
):
    ctx = lax.axis_index("ctx")
    here = lax.axis_index("tensor")
    zh, y, core = ctx >> 3, (ctx >> 1) & 3, ctx & 1
    pp = lax.ppermute
    barrier = lax.optimization_barrier
    q_own, do_own, o_own = queries[0], out_grad[0], attn_out[0]

    half_cols = NH * HD

    def theirs(a):
        return lax.dynamic_slice_in_dim(a, (1 - core) * half_cols, half_cols, axis=1)

    def line_of(pair):
        return [pair] + [pp(pair, "ctx", y_perm(-k)) for k in range(1, 4)]

    def both_cores(line):
        return line + [pp(jnp.concatenate(line), "ctx", CORE_PERM)]

    def with_zhi(own):
        return jnp.concatenate([own, pp(own, "ctx", ZHI_PERM)])

    k_line = line_of(with_zhi(key_heads[0]))
    q_got = pp(theirs(q_own), "ctx", CORE_PERM)
    v_pair = with_zhi(value_heads[0])
    do_o_got = pp(jnp.stack([theirs(do_own), theirs(o_own)]), "ctx", CORE_PERM)

    blocks = jnp.arange(block_order.shape[0], dtype=jnp.int32)
    owner = blocks >> 1
    flip = ((owner & 1) ^ core) * 8
    from_slot = (flip + ((((owner >> 1) - y) & 3) * 2) + ((owner >> 3) ^ zh)) * 2 + (blocks & 1)
    to_slot = (flip + (owner >> 1)) * 2 + (blocks & 1)
    at_place = block_order[None, :] == blocks[:, None]
    pos = jnp.sum(jnp.where(at_place, from_slot[None, :], 0), axis=1)
    to = jnp.sum(jnp.where(at_place, to_slot[None, :], 0), axis=1)
    mine = jnp.stack([2 * ctx, 2 * ctx + 1, 2 * (ctx ^ 1), 2 * (ctx ^ 1) + 1])
    rank = jnp.sum(jnp.where(blocks[None, :] == mine[:, None], block_order[None, :], 0), axis=1)
    core1, here1 = core.reshape(1), here.reshape(1)

    cols = normed_input.shape[2] // 8
    x_own = normed_input[0]
    x_keep = lax.dynamic_slice_in_dim(x_own, core * NX * cols, NX * cols, axis=1)
    x_got = pp(
        lax.dynamic_slice_in_dim(x_own, (1 - core) * NX * cols, NX * cols, axis=1), "ctx", CORE_PERM
    )

    def x_for(dx):
        at = ((here + dx) & 3) * cols
        return jnp.stack([lax.dynamic_slice_in_dim(a, at, cols, axis=1) for a in (x_keep, x_got)])

    def w_for(dx):
        at = (core * NX + ((here - dx) & 3)) * cols
        return jnp.stack(
            [lax.dynamic_slice_in_dim(w, at, cols, axis=0) for w in (key_weight, value_weight)]
        )

    x_near = [x_for(d) for d in range(NX)]
    w_near = [w_for(d) for d in range(NX)]
    k_line, v_pair, x_near, w_near, do_o_got = barrier((k_line, v_pair, x_near, w_near, do_o_got))
    k_slots = both_cores(k_line)
    v_line = line_of(v_pair)
    w_slots = w_near[:1] + [pp(w_near[d], "tensor", x_perm(-d)) for d in range(1, NX)]
    x_slots = x_near[:1] + [pp(x_near[d], "tensor", x_perm(d)) for d in range(1, NX)]

    lse = softmax_stats(rank, pos, core1, q_own, q_got, k_slots)
    lse, v_line, w_slots = barrier((lse, v_line, w_slots))
    v_slots = both_cores(v_line)
    dq_keep, dq_send, dkv0, dkv1 = attention_grads(
        rank, pos, to, core1, lse, q_own, q_got, do_own, o_own, do_o_got, k_slots, v_slots
    )
    dkv1, x_slots = barrier((dkv1, x_slots))

    rows = key_heads.shape[1]
    x_turned = turn_columns(x_slots)
    chip = summed(dkv0, pp(dkv1, "ctx", CORE_PERM)).astype(BF).reshape(8, rows, 2 * HD)
    terms = lax.all_to_all(chip, "ctx", 0, 0, axis_index_groups=CHIP_GROUPS, tiled=True)
    grads = jnp.sum(terms.astype(F32), axis=0).astype(BF)

    dq_got = pp(dq_send, "ctx", CORE_PERM)
    query_grad = jnp.where(
        core == 0,
        jnp.concatenate([dq_keep, dq_got], axis=1),
        jnp.concatenate([dq_got, dq_keep], axis=1),
    )

    g_own = [grads] + [pp(grads, "tensor", x_perm(-dx)) for dx in range(1, NX)]
    g_slots = (g_own, [pp(g, "ctx", CORE_PERM) for g in g_own])

    pieces = proj_parts(here1, g_slots, x_turned)
    pieces, g_slots = barrier((pieces, g_slots))
    pieces = lax.all_to_all(
        pieces, ("dp", "ctx"), 0, 0, axis_index_groups=ALL_CHIP_GROUPS, tiled=True
    )
    outs = input_blocks(here1, g_slots, w_slots)
    got = [
        outs[n] if n == 0 else pp(outs[n], ("ctx", "tensor"), cx_perm(n // NX, n % NX))
        for n in range(8)
    ]
    proj = pp(
        jnp.sum(pieces.astype(F32), axis=0).astype(BF), ("dp", "ctx", "tensor"), home_perm()
    )
    input_grad = place(jnp.stack([core, here]), got)
    return (query_grad[None], input_grad[None], proj[:, :HD], proj[:, HD:])


def solution(mesh):
    in_specs = (
        P("dp", ("ctx", "tensor"), None),
        P("dp", "ctx", "tensor"),
        P("dp", "ctx", "tensor"),
        P("dp", "ctx", "tensor"),
        P("dp", "ctx", "tensor"),
        P("dp", "ctx", "tensor"),
        P(None, "tensor"),
        P(None, "tensor"),
        P(),
    )
    out_specs = (
        P("dp", "ctx", "tensor"),
        P("dp", ("ctx", "tensor"), None),
        P(("dp", "ctx"), "tensor"),
        P(("dp", "ctx"), "tensor"),
    )
    return jax.shard_map(
        per_device, mesh=mesh, in_specs=in_specs, out_specs=out_specs, check_vma=False
    )
```

```python
import functools

import jax
import jax.numpy as jnp
from jax import lax
from jax.experimental import pallas as pl
from jax.experimental.pallas import tpu as pltpu
from jax.sharding import PartitionSpec as P

HD = 128
HQ = 6
NH = 3
BLK = 256
NX = 4
LOG2E = 1.4426950408889634
NEG = -1e30
SC = HD ** (-0.5)
F32 = jnp.float32
BF = jnp.bfloat16

CORE_PERM = [(i, i ^ 1) for i in range(16)]
ZHI_PERM = [(i, i ^ 8) for i in range(16)]
CHIP_GROUPS = [[2 * i + c for i in range(8)] for c in range(2)]
ALL_CHIP_GROUPS = [[2 * i + c for i in range(16)] for c in range(2)]


def y_perm(by):
    return [(i, (i & 9) | (((((i >> 1) & 3) + by) & 3) << 1)) for i in range(16)]


def x_perm(by):
    return [(i, (i + by) % NX) for i in range(NX)]


def cx_perm(flip, by):
    return [(i, (((i >> 2) ^ flip) << 2) | ((i + by) & 3)) for i in range(64)]


def load_blocks(refs, dst, place_ref, sem, at):
    copies = []
    n = 0
    for ref in refs:
        for row in range(0, ref.shape[0], HD):
            for col in range(0, ref.shape[1], BLK):
                to = pl.ds(pl.multiple_of(place_ref[n] * BLK, BLK), BLK)
                src = ref.at[pl.ds(row, HD), pl.ds(col, BLK)]
                copies.append(pltpu.make_async_copy(src, dst.at[:, to], sem.at[at + n]))
                copies[-1].start()
                n += 1
    return copies


def turn_kernel(core_ref, q_own, q_got, do_own, o_own, do_o_got, qaug, doaug, qT, doT):
    blocks = q_own.shape[0] // BLK
    base = core_ref[0] * (NH * HD)
    lane = lax.broadcasted_iota(jnp.int32, (BLK, HD), 1)
    for b in range(2 * blocks):
        for h in range(NH):
            w = pl.ds(h * BLK, BLK)
            r = pl.ds((b % blocks) * BLK, BLK)
            if b < blocks:
                c = pl.ds(pl.multiple_of(base + h * HD, HD), HD)
                q, do, o = q_own[r, c], do_own[r, c], o_own[r, c]
            else:
                c = pl.ds(h * HD, HD)
                q, do, o = q_got[r, c], do_o_got[0, r, c], do_o_got[1, r, c]
            scaled = q.astype(F32) * (SC * LOG2E)
            hi = scaled.astype(BF)
            qaug[b, w, 0:HD] = hi
            qaug[b, w, HD : 2 * HD] = (scaled - hi.astype(F32)).astype(BF)
            qT[b, :, w] = q.T
            doT[b, :, w] = do.T
            doaug[b, w, 0:HD] = do
            d = -jnp.sum(do.astype(F32) * o.astype(F32), axis=1, keepdims=True)
            d1 = d.astype(BF).astype(F32)
            d2 = (d - d1).astype(BF).astype(F32)
            d3 = d - d1 - d2
            aug = jnp.where(lane == 0, d1, jnp.where(lane == 1, d2, jnp.where(lane == 2, d3, 0.0)))
            doaug[b, w, HD : 2 * HD] = aug.astype(BF)


def causal():
    qry_i = lax.broadcasted_iota(jnp.int32, (NH * BLK, BLK), 0) % BLK
    key_i = lax.broadcasted_iota(jnp.int32, (NH * BLK, BLK), 1)
    return key_i <= qry_i


def over_keys(rank, step):
    def four(j, _):
        step(j * (4 * BLK), 4 * BLK, False)
        return 0

    lax.fori_loop(0, rank // 4, four, 0)
    done = 4 * (rank // 4)

    @pl.when(rank - done >= 2)
    def _():
        step(done * BLK, 2 * BLK, False)

    @pl.when(rank % 2 == 1)
    def _():
        step((rank - 1) * BLK, BLK, False)

    step(rank * BLK, BLK, True)


def stats_kernel(rank_ref, place_ref, qaug_hbm, *rest, n_slots):
    k_refs, lse = rest[:n_slots], rest[n_slots]
    kT, qaug, m_s, l_s, sem = rest[n_slots + 1 :]
    nblk = kT.shape[1] // BLK
    load_q = pltpu.make_async_copy(qaug_hbm, qaug, sem.at[2 * nblk])
    load_q.start()
    copies = load_blocks(k_refs, kT.at[0:HD, :], place_ref, sem, 0)
    copies += load_blocks(k_refs, kT.at[HD : 2 * HD, :], place_ref, sem, nblk)
    load_q.wait()
    for c in copies:
        c.wait()
    allowed = causal()

    def q_loop(b, _):
        def step(at, rows, diag):
            keys = kT[:, pl.ds(pl.multiple_of(at, BLK), rows)]
            s = jnp.dot(qaug[b], keys, preferred_element_type=F32)
            if diag:
                s = jnp.where(allowed, s, NEG)
            parts = [s[:, i : i + HD] for i in range(0, rows, HD)]
            m0 = m_s[...]
            m1 = m0
            for part in parts:
                m1 = jnp.maximum(m1, part)
            total = l_s[...] * jnp.exp2(m0 - m1)
            for part in parts:
                total = total + jnp.exp2(part - m1)
            l_s[...] = total
            m_s[...] = m1

        m_s[...] = jnp.full(m_s.shape, NEG, F32)
        l_s[...] = jnp.zeros(l_s.shape, F32)
        over_keys(rank_ref[b], step)
        m = m_s[...]
        top = jnp.max(m, axis=1, keepdims=True)
        total = jnp.sum(l_s[...] * jnp.exp2(m - top), axis=1, keepdims=True)
        lse[b] = jnp.broadcast_to(top + jnp.log2(total), m.shape)
        return 0

    lax.fori_loop(0, qaug.shape[0], q_loop, 0)


def grads_kernel(rank_ref, place_ref, v_place_ref, out_place_ref, *rest, n_k, n_v):
    sides, k_refs, v_refs = rest[:5], rest[5 : 5 + n_k], rest[5 + n_k : 5 + n_k + n_v]
    rest = rest[5 + n_k + n_v :]
    dq_out, dkv_out = rest[:2], rest[2:4]
    kT, vT, kn, dq, dkvT, dqs, dkvs, lse, qaug, doaug, qT, doT, sem, sem_side, sem_out = rest[4:]
    nq = qaug.shape[0]
    nblk = kT.shape[1] // BLK
    loads = []
    for n, (src, dst) in enumerate(zip(sides, (lse, qaug, doaug, qT, doT))):
        loads.append(pltpu.make_async_copy(src, dst, sem_side.at[n]))
    copies = load_blocks(k_refs, kT.at[0:HD, :], place_ref, sem, 0)
    copies += load_blocks(k_refs, kT.at[HD : 2 * HD, :], place_ref, sem, nblk)
    v_copies = load_blocks(v_refs, vT.at[0:HD, :], v_place_ref, sem, 2 * nblk)
    for c in loads:
        c.start()
    row = lax.broadcasted_iota(jnp.int32, (HD, BLK), 0)
    ones = jnp.where(row < 3, 1.0, 0.0).astype(BF)

    def init(i, _):
        r = pl.ds(pl.multiple_of(i * BLK, BLK), BLK)
        vT[HD : 2 * HD, r] = ones
        dkvT[:, r] = jnp.zeros((2 * HD, BLK), F32)
        return 0

    lax.fori_loop(0, nblk, init, 0)
    for c in copies:
        c.wait()

    def turn(i, _):
        r = pl.ds(pl.multiple_of(i * BLK, BLK), BLK)
        kn[r, :] = kT[0:HD, r].T
        return 0

    lax.fori_loop(0, nblk, turn, 0)
    for c in v_copies + loads:
        c.wait()
    allowed = causal()

    def q_loop(b, _):
        def step(at, rows, diag):
            r = pl.ds(pl.multiple_of(at, BLK), rows)
            total = jnp.concatenate([lse[b]] * (rows // HD), axis=1)
            p = jnp.exp2(jnp.dot(qaug[b], kT[:, r], preferred_element_type=F32) - total)
            if diag:
                p = jnp.where(allowed, p, 0.0)
            dp = jnp.dot(doaug[b], vT[:, r], preferred_element_type=F32)
            p16 = p.astype(BF)
            ds16 = (p * dp).astype(BF)
            dkvT[HD : 2 * HD, r] += jnp.dot(doT[b], p16, preferred_element_type=F32)
            dkvT[0:HD, r] += jnp.dot(qT[b], ds16, preferred_element_type=F32)
            dq[...] += jnp.dot(ds16, kn[r, :], preferred_element_type=F32)

        dq[...] = jnp.zeros(dq.shape, F32)
        over_keys(rank_ref[b], step)
        for h in range(NH):
            dqs[b, :, pl.ds(h * HD, HD)] = (dq[pl.ds(h * BLK, BLK), :] * SC).astype(BF)
        return 0

    lax.fori_loop(0, nq, q_loop, 0)
    stores = []
    for b in range(nq):
        dst = dq_out[b // (nq // 2)].at[pl.ds((b % (nq // 2)) * BLK, BLK), :]
        stores.append(pltpu.make_async_copy(dqs.at[b], dst, sem_out.at[b]))
        stores[-1].start()
    slots = nblk // 4
    for side in (1, 0):
        for i in range(slots):
            for n in range(2):
                at = out_place_ref[side * (nblk // 2) + 2 * i + n]
                c = pl.ds(pl.multiple_of(at * BLK, BLK), BLK)
                m = side * slots + i
                dkvs[m, 0:HD, pl.ds(n * BLK, BLK)] = (dkvT[0:HD, c] * SC).astype(BF)
                dkvs[m, HD : 2 * HD, pl.ds(n * BLK, BLK)] = dkvT[HD : 2 * HD, c].astype(BF)
            stores.append(pltpu.make_async_copy(dkvs.at[m], dkv_out[side].at[i], sem_out.at[nq + m]))
            stores[-1].start()
    for c in stores:
        c.wait()


VM = pl.BlockSpec(memory_space=pltpu.VMEM)
SM = pl.BlockSpec(memory_space=pltpu.SMEM)
HB = pl.BlockSpec(memory_space=pl.ANY)


BIG = 60 * 1024 * 1024


def turned(core, q, q_got, do, o, do_o_got):
    nq = 2 * q.shape[0] // BLK
    W = NH * BLK
    return pl.pallas_call(
        turn_kernel,
        out_shape=(
            jax.ShapeDtypeStruct((nq, W, 2 * HD), BF),
            jax.ShapeDtypeStruct((nq, W, 2 * HD), BF),
            jax.ShapeDtypeStruct((nq, HD, W), BF),
            jax.ShapeDtypeStruct((nq, HD, W), BF),
        ),
        in_specs=[SM] + [VM] * 5,
        out_specs=(VM,) * 4,
        compiler_params=pltpu.CompilerParams(vmem_limit_bytes=BIG),
        name="turned_queries",
    )(core, q, q_got, do, o, do_o_got)


def softmax_stats(rank, place, qaug, k_slots):
    nq, W, _ = qaug.shape
    nblk = place.shape[0]
    keys = nblk * BLK
    n = len(k_slots)
    pairs = 66 * W * BLK
    return pl.pallas_call(
        functools.partial(stats_kernel, n_slots=n),
        out_shape=jax.ShapeDtypeStruct((nq, W, HD), F32),
        in_specs=[SM] * 2 + [HB] * (1 + n),
        out_specs=VM,
        scratch_shapes=[
            pltpu.VMEM((2 * HD, keys), BF),
            pltpu.VMEM((nq, W, 2 * HD), BF),
            pltpu.VMEM((W, HD), F32),
            pltpu.VMEM((W, HD), F32),
            pltpu.SemaphoreType.DMA((2 * nblk + 1,)),
        ],
        compiler_params=pltpu.CompilerParams(vmem_limit_bytes=BIG),
        cost_estimate=pl.CostEstimate(
            flops=16 * pairs * HD, bytes_accessed=4 * 1024 * 1024, transcendentals=pairs
        ),
        name="softmax_stats",
    )(rank, place, qaug, *k_slots)


def attention_grads(rank, places, lse, qaug, doaug, qT, doT, k_slots, v_slots):
    nq, W, _ = qaug.shape
    half = nq * BLK // 2
    nblk = places.shape[1]
    keys = nblk * BLK
    n = len(k_slots)
    pairs = 66 * W * BLK
    return pl.pallas_call(
        functools.partial(grads_kernel, n_k=n, n_v=len(v_slots)),
        out_shape=(
            jax.ShapeDtypeStruct((half, NH * HD), BF),
            jax.ShapeDtypeStruct((half, NH * HD), BF),
            jax.ShapeDtypeStruct((nblk // 4, 2 * HD, 2 * BLK), BF),
            jax.ShapeDtypeStruct((nblk // 4, 2 * HD, 2 * BLK), BF),
        ),
        in_specs=[SM] * 4 + [HB] * (5 + n + len(v_slots)),
        out_specs=(HB,) * 4,
        scratch_shapes=[
            pltpu.VMEM((2 * HD, keys), BF),
            pltpu.VMEM((2 * HD, keys), BF),
            pltpu.VMEM((keys, HD), BF),
            pltpu.VMEM((W, HD), F32),
            pltpu.VMEM((2 * HD, keys), F32),
            pltpu.VMEM((nq, BLK, NH * HD), BF),
            pltpu.VMEM((nblk // 2, 2 * HD, 2 * BLK), BF),
            pltpu.VMEM(lse.shape, F32),
            pltpu.VMEM(qaug.shape, BF),
            pltpu.VMEM(doaug.shape, BF),
            pltpu.VMEM(qT.shape, BF),
            pltpu.VMEM(doT.shape, BF),
            pltpu.SemaphoreType.DMA((3 * nblk,)),
            pltpu.SemaphoreType.DMA((5,)),
            pltpu.SemaphoreType.DMA((nq + nblk // 2,)),
        ],
        compiler_params=pltpu.CompilerParams(vmem_limit_bytes=BIG),
        cost_estimate=pl.CostEstimate(
            flops=32 * pairs * HD, bytes_accessed=16 * 1024 * 1024, transcendentals=pairs
        ),
        name="attention_grads",
    )(rank, *places, lse, qaug, doaug, qT, doT, *k_slots, *v_slots)


def load_grads(here, g_refs, g_all, sem):
    copies = []
    rows = g_refs[0][0].shape[0]
    for cs in range(2):
        for dx in range(NX):
            at = ((here + dx) % NX) * (2 * HD)
            dst = g_all.at[pl.ds(cs * rows, rows), pl.ds(pl.multiple_of(at, 2 * HD), 2 * HD)]
            copies.append(pltpu.make_async_copy(g_refs[cs][dx], dst, sem.at[cs * NX + dx]))
            copies[-1].start()
    return copies


def input_kernel(here_ref, *rest):
    here = here_ref[0]
    g_refs = (rest[0:4], rest[4:8])
    w_refs, outs = rest[8:12], rest[12:20]
    g_all, w_all, result, sem, sem_w = rest[20:]
    copies = load_grads(here, g_refs, g_all, sem)
    for n in range(8):
        at = ((here + n // 2) % NX) * (2 * HD) + (n % 2) * HD
        dst = w_all.at[:, pl.ds(pl.multiple_of(at, HD), HD)]
        copies.append(pltpu.make_async_copy(w_refs[n // 2].at[n % 2], dst, sem_w.at[n]))
        copies[-1].start()
    for c in copies:
        c.wait()
    cols = w_all.shape[0]
    for at in range(0, cols, 2 * HD):
        c = pl.ds(at, min(2 * HD, cols - at))
        block = lax.dot_general(
            g_all[...], w_all[c, :], (((1,), (1,)), ((), ())), preferred_element_type=F32
        ).astype(BF)
        result[:, c] = block
    for n, out in enumerate(outs):
        row = (n // NX) * (NX * HD) + ((here + n) % NX) * HD
        out[...] = result[pl.ds(pl.multiple_of(row, HD), HD), :]


def input_blocks(here, g_slots, w_slots):
    cols = w_slots[0].shape[1]
    return pl.pallas_call(
        input_kernel,
        out_shape=tuple(jax.ShapeDtypeStruct((HD, cols), BF) for _ in range(8)),
        in_specs=[SM] + [HB] * 12,
        out_specs=(VM,) * 8,
        scratch_shapes=[
            pltpu.VMEM((8 * HD, 8 * HD), BF),
            pltpu.VMEM((cols, 8 * HD), BF),
            pltpu.VMEM((8 * HD, cols), BF),
            pltpu.SemaphoreType.DMA((8,)),
            pltpu.SemaphoreType.DMA((8,)),
        ],
        compiler_params=pltpu.CompilerParams(vmem_limit_bytes=BIG),
        cost_estimate=pl.CostEstimate(
            flops=2 * 1024 * 1024 * cols, bytes_accessed=7 * 1024 * 1024, transcendentals=0
        ),
        name="input_blocks",
    )(here, *g_slots[0], *g_slots[1], *w_slots)


def proj_kernel(x_ref, g0, g1, out, x_all, g_all, total, sem_x, sem_g, sem_out):
    rows = g0.shape[0]
    pieces, part = out.shape[0], out.shape[1]
    chunk = x_all.shape[0] // 4
    loads = []
    for n, g in enumerate((g0, g1)):
        loads.append(pltpu.make_async_copy(g, g_all.at[pl.ds(n * rows, rows), :], sem_g.at[n]))
        loads[-1].start()
    x_loads = []
    for j in range(4):
        r = pl.ds(j * chunk, chunk)
        for n in range(8):
            src = x_ref.at[n % NX, n // NX, r, :]
            dst = x_all.at[r, pl.ds(n * HD, HD)]
            x_loads.append(pltpu.make_async_copy(src, dst, sem_x.at[j * 8 + n]))
            x_loads[-1].start()
    for c in loads:
        c.wait()
    stores = []
    for j in range(4):
        for c in x_loads[j * 8 : j * 8 + 8]:
            c.wait()
        halves = [pl.ds(j * chunk + n * (chunk // 2), chunk // 2) for n in range(2)]
        sums = [jnp.dot(x_all[h, :], g_all[...], preferred_element_type=F32) for h in halves]
        for h, part_sum in zip(halves, sums):
            total[h, :] = part_sum.astype(BF)
        for n in range(j * pieces // 4, (j + 1) * pieces // 4):
            src = total.at[pl.ds(n * part, part), :]
            stores.append(pltpu.make_async_copy(src, out.at[n], sem_out.at[n]))
            stores[-1].start()
    for c in stores:
        c.wait()


def proj_parts(x_turned, g0, g1):
    cols = x_turned.shape[2]
    return pl.pallas_call(
        proj_kernel,
        out_shape=jax.ShapeDtypeStruct((16, cols // 16, 2 * HD), BF),
        in_specs=[HB] * 3,
        out_specs=HB,
        scratch_shapes=[
            pltpu.VMEM((cols, 8 * HD), BF),
            pltpu.VMEM((8 * HD, 2 * HD), BF),
            pltpu.VMEM((cols, 2 * HD), BF),
            pltpu.SemaphoreType.DMA((32,)),
            pltpu.SemaphoreType.DMA((2,)),
            pltpu.SemaphoreType.DMA((16,)),
        ],
        compiler_params=pltpu.CompilerParams(vmem_limit_bytes=BIG),
        cost_estimate=pl.CostEstimate(
            flops=2 * 1024 * 256 * cols, bytes_accessed=13 * 1024 * 1024, transcendentals=0
        ),
        name="proj_parts",
    )(x_turned, g0, g1)


def place_kernel(where_ref, *rest):
    core, here = where_ref[0], where_ref[1]
    parts, out = rest[:8], rest[8]
    cols = parts[0].shape[1]
    for cs in range(2):
        for dx in range(NX):
            at = ((core + cs) % 2) * (NX * cols) + ((here - dx + NX) % NX) * cols
            out[:, pl.ds(pl.multiple_of(at, HD), cols)] = parts[cs * NX + dx][...]


def place(where, parts):
    rows, cols = parts[0].shape
    return pl.pallas_call(
        place_kernel,
        out_shape=jax.ShapeDtypeStruct((rows, 8 * cols), BF),
        in_specs=[SM] + [VM] * 8,
        out_specs=VM,
        compiler_params=pltpu.CompilerParams(vmem_limit_bytes=BIG),
        name="place_columns",
    )(where, *parts)


def summed(*terms):
    total = terms[0].astype(F32)
    for term in terms[1:]:
        total = total + term.astype(F32)
    return total


def per_device(
    normed_input,
    queries,
    key_heads,
    value_heads,
    attn_out,
    out_grad,
    key_weight,
    value_weight,
    block_order,
):
    ctx = lax.axis_index("ctx")
    here = lax.axis_index("tensor")
    zh, y, core = ctx >> 3, (ctx >> 1) & 3, ctx & 1
    pp = lax.ppermute
    barrier = lax.optimization_barrier
    q_own, do_own, o_own = queries[0], out_grad[0], attn_out[0]

    half_cols = NH * HD

    def theirs(a):
        return lax.dynamic_slice_in_dim(a, (1 - core) * half_cols, half_cols, axis=1)

    def to_each(a, n):
        return jnp.broadcast_to(a[None], (n,) + a.shape).reshape(n * a.shape[0], a.shape[1])

    def exchange(a, axes, groups=None):
        return lax.all_to_all(a, axes, 0, 0, axis_index_groups=groups, tiled=True)

    q_got = pp(theirs(q_own), "ctx", CORE_PERM)
    k_mine = exchange(to_each(key_heads[0].T, 8), "ctx", CHIP_GROUPS)
    v_all = lax.all_gather(value_heads[0].T, "ctx", axis=0, tiled=True)
    q_got, do_own, o_own, x_own, key_weight, value_weight = barrier(
        (q_got, do_own, o_own, normed_input[0], key_weight, value_weight)
    )
    do_o_got = pp(jnp.stack([theirs(do_own), theirs(o_own)]), "ctx", CORE_PERM)

    blocks = jnp.arange(block_order.shape[0], dtype=jnp.int32)
    owner = blocks >> 1
    k_slot = ((((owner & 1) ^ core) * 8) + (owner >> 1)) * 2 + (blocks & 1)
    v_slot = blocks
    to_slot = k_slot
    slots = jnp.concatenate([k_slot, v_slot, to_slot]).reshape(3, 1, -1)
    places = jnp.sum(jnp.where(slots == blocks[:, None], block_order, 0), axis=2)
    mine = jnp.stack([2 * ctx, 2 * ctx + 1, 2 * (ctx ^ 1), 2 * (ctx ^ 1) + 1])
    rank = jnp.sum(jnp.where(blocks[None, :] == mine[:, None], block_order[None, :], 0), axis=1)
    core1, here1 = core.reshape(1), here.reshape(1)

    cols = normed_input.shape[2] // 8
    x_halves = x_own.T.reshape(16, 2, -1, x_own.shape[0])

    def x_half(c):
        return lax.dynamic_index_in_dim(x_halves, c, 1, keepdims=False).reshape(NX * cols, -1)

    x_chip = jnp.stack([x_half(core), pp(x_half(1 - core), "ctx", CORE_PERM)])
    w_near = []
    for dx in range(NX):
        at = (core * NX + ((here - dx) & 3)) * cols
        w_near.append(
            jnp.stack([lax.dynamic_slice_in_dim(w, at, cols, axis=0) for w in (key_weight, value_weight)])
        )
    w_slots = w_near[:1] + [pp(w_near[d], "tensor", x_perm(-d)) for d in range(1, NX)]
    qaug, doaug, qT, doT = turned(core1, q_own, q_got, do_own, o_own, do_o_got)
    k_mine, qaug, x_chip = barrier((k_mine, qaug, x_chip))
    x_all = lax.all_gather(x_chip, "tensor")
    k_slots = [k_mine, pp(k_mine, "ctx", CORE_PERM)]
    lse = softmax_stats(rank, places[0], qaug, k_slots)
    lse, w_slots = barrier((lse, w_slots))
    v_slots = [v_all]
    dq_keep, dq_send, dkv0, dkv1 = attention_grads(
        rank, places, lse, qaug, doaug, qT, doT, k_slots, v_slots
    )

    chip = summed(dkv0, pp(dkv1, "ctx", CORE_PERM)).astype(BF)
    terms = lax.all_to_all(chip, "ctx", 0, 0, axis_index_groups=CHIP_GROUPS, tiled=True)
    grads = jnp.sum(terms.astype(F32), axis=0).astype(BF).T

    dq_got = pp(dq_send, "ctx", CORE_PERM)
    query_grad = jnp.where(
        core == 0,
        jnp.concatenate([dq_keep, dq_got], axis=1),
        jnp.concatenate([dq_got, dq_keep], axis=1),
    )

    grads, query_grad = barrier((grads, query_grad))
    g_own = [grads] + [pp(grads, "tensor", x_perm(-dx)) for dx in range(1, NX)]
    g_other = pp(grads, "ctx", CORE_PERM)
    pieces = proj_parts(x_all, grads, g_other)
    pieces, g_own = barrier((pieces, g_own))
    g_slots = (g_own, [g_other] + [pp(g, "ctx", CORE_PERM) for g in g_own[1:]])
    pieces = lax.all_to_all(
        pieces, ("dp", "ctx"), 0, 0, axis_index_groups=ALL_CHIP_GROUPS, tiled=True
    )
    outs = input_blocks(here1, g_slots, w_slots)
    got = [
        outs[n] if n == 0 else pp(outs[n], ("ctx", "tensor"), cx_perm(n // NX, n % NX))
        for n in range(8)
    ]
    input_grad = place(jnp.stack([core, here]), got)
    pieces, input_grad = barrier((pieces, input_grad))
    proj = jnp.sum(pieces.astype(F32), axis=0).astype(BF)
    return (query_grad[None], input_grad[None], proj[:, :HD], proj[:, HD:])


def solution(mesh):
    in_specs = (
        P("dp", ("ctx", "tensor"), None),
        P("dp", "ctx", "tensor"),
        P("dp", "ctx", "tensor"),
        P("dp", "ctx", "tensor"),
        P("dp", "ctx", "tensor"),
        P("dp", "ctx", "tensor"),
        P(None, "tensor"),
        P(None, "tensor"),
        P(),
    )
    out_specs = (
        P("dp", "ctx", "tensor"),
        P("dp", ("ctx", "tensor"), None),
        P(("dp", "ctx"), "tensor"),
        P(("dp", "ctx"), "tensor"),
    )
    return jax.shard_map(
        per_device, mesh=mesh, in_specs=in_specs, out_specs=out_specs, check_vma=False
    )
```

```python
import functools

import jax
import jax.numpy as jnp
from jax import lax
from jax.experimental import pallas as pl
from jax.experimental.pallas import tpu as pltpu
from jax.sharding import PartitionSpec as P

HD = 128
HQ = 6
NH = 3
BLK = 256
NX = 4
LOG2E = 1.4426950408889634
NEG = -1e30
SC = HD ** (-0.5)
F32 = jnp.float32
BF = jnp.bfloat16

CORE_PERM = [(i, i ^ 1) for i in range(16)]
ZHI_PERM = [(i, i ^ 8) for i in range(16)]
CHIP_GROUPS = [[2 * i + c for i in range(8)] for c in range(2)]
ALL_CHIP_GROUPS = [[2 * i + c for i in range(16)] for c in range(2)]


def y_perm(by):
    return [(i, (i & 9) | (((((i >> 1) & 3) + by) & 3) << 1)) for i in range(16)]


def x_perm(by):
    return [(i, (i + by) % NX) for i in range(NX)]


def cx_perm(flip, by):
    return [(i, (((i >> 2) ^ flip) << 2) | ((i + by) & 3)) for i in range(64)]


def load_blocks(refs, dst, place_ref, sem, at):
    copies = []
    n = 0
    for ref in refs:
        for row in range(0, ref.shape[0], HD):
            for col in range(0, ref.shape[1], BLK):
                to = pl.ds(pl.multiple_of(place_ref[n] * BLK, BLK), BLK)
                src = ref.at[pl.ds(row, HD), pl.ds(col, BLK)]
                copies.append(pltpu.make_async_copy(src, dst.at[:, to], sem.at[at + n]))
                copies[-1].start()
                n += 1
    return copies


def turn_kernel(core_ref, q_own, q_got, do_own, o_own, do_o_got, qaug, doaug, qT, doT):
    blocks = q_own.shape[0] // BLK
    base = core_ref[0] * (NH * HD)
    lane = lax.broadcasted_iota(jnp.int32, (BLK, HD), 1)
    for b in range(2 * blocks):
        for h in range(NH):
            w = pl.ds(h * BLK, BLK)
            r = pl.ds((b % blocks) * BLK, BLK)
            if b < blocks:
                c = pl.ds(pl.multiple_of(base + h * HD, HD), HD)
                q, do, o = q_own[r, c], do_own[r, c], o_own[r, c]
            else:
                c = pl.ds(h * HD, HD)
                q, do, o = q_got[r, c], do_o_got[0, r, c], do_o_got[1, r, c]
            scaled = q.astype(F32) * (SC * LOG2E)
            hi = scaled.astype(BF)
            qaug[b, w, 0:HD] = hi
            qaug[b, w, HD : 2 * HD] = (scaled - hi.astype(F32)).astype(BF)
            qT[b, :, w] = q.T
            doT[b, :, w] = do.T
            doaug[b, w, 0:HD] = do
            d = -jnp.sum(do.astype(F32) * o.astype(F32), axis=1, keepdims=True)
            d1 = d.astype(BF).astype(F32)
            d2 = (d - d1).astype(BF).astype(F32)
            d3 = d - d1 - d2
            aug = jnp.where(lane == 0, d1, jnp.where(lane == 1, d2, jnp.where(lane == 2, d3, 0.0)))
            doaug[b, w, HD : 2 * HD] = aug.astype(BF)


def causal():
    qry_i = lax.broadcasted_iota(jnp.int32, (NH * BLK, BLK), 0) % BLK
    key_i = lax.broadcasted_iota(jnp.int32, (NH * BLK, BLK), 1)
    return key_i <= qry_i


def over_keys(rank, step):
    def four(j, _):
        step(j * (4 * BLK), 4 * BLK, False)
        return 0

    lax.fori_loop(0, rank // 4, four, 0)
    done = 4 * (rank // 4)

    @pl.when(rank - done >= 2)
    def _():
        step(done * BLK, 2 * BLK, False)

    @pl.when(rank % 2 == 1)
    def _():
        step((rank - 1) * BLK, BLK, False)

    step(rank * BLK, BLK, True)


def stats_kernel(rank_ref, place_ref, qaug_hbm, *rest, n_slots):
    k_refs, lse = rest[:n_slots], rest[n_slots]
    kT, qaug, m_s, l_s, sem = rest[n_slots + 1 :]
    nblk = kT.shape[1] // BLK
    load_q = pltpu.make_async_copy(qaug_hbm, qaug, sem.at[2 * nblk])
    load_q.start()
    copies = load_blocks(k_refs, kT.at[0:HD, :], place_ref, sem, 0)
    copies += load_blocks(k_refs, kT.at[HD : 2 * HD, :], place_ref, sem, nblk)
    load_q.wait()
    for c in copies:
        c.wait()
    allowed = causal()

    def q_loop(b, _):
        def step(at, rows, diag):
            keys = kT[:, pl.ds(pl.multiple_of(at, BLK), rows)]
            s = jnp.dot(qaug[b], keys, preferred_element_type=F32)
            if diag:
                s = jnp.where(allowed, s, NEG)
            parts = [s[:, i : i + HD] for i in range(0, rows, HD)]
            m0 = m_s[...]
            m1 = m0
            for part in parts:
                m1 = jnp.maximum(m1, part)
            total = l_s[...] * jnp.exp2(m0 - m1)
            for part in parts:
                total = total + jnp.exp2(part - m1)
            l_s[...] = total
            m_s[...] = m1

        m_s[...] = jnp.full(m_s.shape, NEG, F32)
        l_s[...] = jnp.zeros(l_s.shape, F32)
        over_keys(rank_ref[b], step)
        m = m_s[...]
        top = jnp.max(m, axis=1, keepdims=True)
        total = jnp.sum(l_s[...] * jnp.exp2(m - top), axis=1, keepdims=True)
        lse[b] = jnp.broadcast_to(top + jnp.log2(total), m.shape)
        return 0

    lax.fori_loop(0, qaug.shape[0], q_loop, 0)


def grads_kernel(rank_ref, place_ref, v_place_ref, out_place_ref, *rest, n_k, n_v):
    sides, k_refs, v_refs = rest[:5], rest[5 : 5 + n_k], rest[5 + n_k : 5 + n_k + n_v]
    rest = rest[5 + n_k + n_v :]
    dq_out, dkv_out = rest[:2], rest[2:4]
    kT, vT, kn, dq, dkvT, dqs, dkvs, lse, qaug, doaug, qT, doT, sem, sem_side, sem_out = rest[4:]
    nq = qaug.shape[0]
    nblk = kT.shape[1] // BLK
    loads = []
    for n, (src, dst) in enumerate(zip(sides, (lse, qaug, doaug, qT, doT))):
        loads.append(pltpu.make_async_copy(src, dst, sem_side.at[n]))
    copies = load_blocks(k_refs, kT.at[0:HD, :], place_ref, sem, 0)
    copies += load_blocks(k_refs, kT.at[HD : 2 * HD, :], place_ref, sem, nblk)
    v_copies = load_blocks(v_refs, vT.at[0:HD, :], v_place_ref, sem, 2 * nblk)
    for c in loads:
        c.start()
    row = lax.broadcasted_iota(jnp.int32, (HD, BLK), 0)
    ones = jnp.where(row < 3, 1.0, 0.0).astype(BF)

    def init(i, _):
        r = pl.ds(pl.multiple_of(i * BLK, BLK), BLK)
        vT[HD : 2 * HD, r] = ones
        dkvT[:, r] = jnp.zeros((2 * HD, BLK), F32)
        return 0

    lax.fori_loop(0, nblk, init, 0)
    for c in copies:
        c.wait()

    def turn(i, _):
        r = pl.ds(pl.multiple_of(i * BLK, BLK), BLK)
        kn[r, :] = kT[0:HD, r].T
        return 0

    lax.fori_loop(0, nblk, turn, 0)
    for c in v_copies + loads:
        c.wait()
    allowed = causal()

    def q_loop(b, _):
        def step(at, rows, diag):
            r = pl.ds(pl.multiple_of(at, BLK), rows)
            total = jnp.concatenate([lse[b]] * (rows // HD), axis=1)
            p = jnp.exp2(jnp.dot(qaug[b], kT[:, r], preferred_element_type=F32) - total)
            if diag:
                p = jnp.where(allowed, p, 0.0)
            dp = jnp.dot(doaug[b], vT[:, r], preferred_element_type=F32)
            p16 = p.astype(BF)
            ds16 = (p * dp).astype(BF)
            dkvT[HD : 2 * HD, r] += jnp.dot(doT[b], p16, preferred_element_type=F32)
            dkvT[0:HD, r] += jnp.dot(qT[b], ds16, preferred_element_type=F32)
            dq[...] += jnp.dot(ds16, kn[r, :], preferred_element_type=F32)

        dq[...] = jnp.zeros(dq.shape, F32)
        over_keys(rank_ref[b], step)
        for h in range(NH):
            dqs[b, :, pl.ds(h * HD, HD)] = (dq[pl.ds(h * BLK, BLK), :] * SC).astype(BF)
        return 0

    lax.fori_loop(0, nq, q_loop, 0)
    stores = []
    for b in range(nq):
        dst = dq_out[b // (nq // 2)].at[pl.ds((b % (nq // 2)) * BLK, BLK), :]
        stores.append(pltpu.make_async_copy(dqs.at[b], dst, sem_out.at[b]))
        stores[-1].start()
    slots = nblk // 4
    for side in (1, 0):
        for i in range(slots):
            for n in range(2):
                at = out_place_ref[side * (nblk // 2) + 2 * i + n]
                c = pl.ds(pl.multiple_of(at * BLK, BLK), BLK)
                m = side * slots + i
                dkvs[m, 0:HD, pl.ds(n * BLK, BLK)] = (dkvT[0:HD, c] * SC).astype(BF)
                dkvs[m, HD : 2 * HD, pl.ds(n * BLK, BLK)] = dkvT[HD : 2 * HD, c].astype(BF)
            stores.append(pltpu.make_async_copy(dkvs.at[m], dkv_out[side].at[i], sem_out.at[nq + m]))
            stores[-1].start()
    for c in stores:
        c.wait()


VM = pl.BlockSpec(memory_space=pltpu.VMEM)
SM = pl.BlockSpec(memory_space=pltpu.SMEM)
HB = pl.BlockSpec(memory_space=pl.ANY)


BIG = 60 * 1024 * 1024


def turned(core, q, q_got, do, o, do_o_got):
    nq = 2 * q.shape[0] // BLK
    W = NH * BLK
    return pl.pallas_call(
        turn_kernel,
        out_shape=(
            jax.ShapeDtypeStruct((nq, W, 2 * HD), BF),
            jax.ShapeDtypeStruct((nq, W, 2 * HD), BF),
            jax.ShapeDtypeStruct((nq, HD, W), BF),
            jax.ShapeDtypeStruct((nq, HD, W), BF),
        ),
        in_specs=[SM] + [VM] * 5,
        out_specs=(VM,) * 4,
        compiler_params=pltpu.CompilerParams(vmem_limit_bytes=BIG),
        name="turned_queries",
    )(core, q, q_got, do, o, do_o_got)


def softmax_stats(rank, place, qaug, k_slots):
    nq, W, _ = qaug.shape
    nblk = place.shape[0]
    keys = nblk * BLK
    n = len(k_slots)
    pairs = 66 * W * BLK
    return pl.pallas_call(
        functools.partial(stats_kernel, n_slots=n),
        out_shape=jax.ShapeDtypeStruct((nq, W, HD), F32),
        in_specs=[SM] * 2 + [HB] * (1 + n),
        out_specs=VM,
        scratch_shapes=[
            pltpu.VMEM((2 * HD, keys), BF),
            pltpu.VMEM((nq, W, 2 * HD), BF),
            pltpu.VMEM((W, HD), F32),
            pltpu.VMEM((W, HD), F32),
            pltpu.SemaphoreType.DMA((2 * nblk + 1,)),
        ],
        compiler_params=pltpu.CompilerParams(vmem_limit_bytes=BIG),
        cost_estimate=pl.CostEstimate(
            flops=16 * pairs * HD, bytes_accessed=4 * 1024 * 1024, transcendentals=pairs
        ),
        name="softmax_stats",
    )(rank, place, qaug, *k_slots)


def attention_grads(rank, places, lse, qaug, doaug, qT, doT, k_slots, v_slots):
    nq, W, _ = qaug.shape
    half = nq * BLK // 2
    nblk = places.shape[1]
    keys = nblk * BLK
    n = len(k_slots)
    pairs = 66 * W * BLK
    return pl.pallas_call(
        functools.partial(grads_kernel, n_k=n, n_v=len(v_slots)),
        out_shape=(
            jax.ShapeDtypeStruct((half, NH * HD), BF),
            jax.ShapeDtypeStruct((half, NH * HD), BF),
            jax.ShapeDtypeStruct((nblk // 4, 2 * HD, 2 * BLK), BF),
            jax.ShapeDtypeStruct((nblk // 4, 2 * HD, 2 * BLK), BF),
        ),
        in_specs=[SM] * 4 + [HB] * (5 + n + len(v_slots)),
        out_specs=(HB,) * 4,
        scratch_shapes=[
            pltpu.VMEM((2 * HD, keys), BF),
            pltpu.VMEM((2 * HD, keys), BF),
            pltpu.VMEM((keys, HD), BF),
            pltpu.VMEM((W, HD), F32),
            pltpu.VMEM((2 * HD, keys), F32),
            pltpu.VMEM((nq, BLK, NH * HD), BF),
            pltpu.VMEM((nblk // 2, 2 * HD, 2 * BLK), BF),
            pltpu.VMEM(lse.shape, F32),
            pltpu.VMEM(qaug.shape, BF),
            pltpu.VMEM(doaug.shape, BF),
            pltpu.VMEM(qT.shape, BF),
            pltpu.VMEM(doT.shape, BF),
            pltpu.SemaphoreType.DMA((3 * nblk,)),
            pltpu.SemaphoreType.DMA((5,)),
            pltpu.SemaphoreType.DMA((nq + nblk // 2,)),
        ],
        compiler_params=pltpu.CompilerParams(vmem_limit_bytes=BIG),
        cost_estimate=pl.CostEstimate(
            flops=32 * pairs * HD, bytes_accessed=16 * 1024 * 1024, transcendentals=pairs
        ),
        name="attention_grads",
    )(rank, *places, lse, qaug, doaug, qT, doT, *k_slots, *v_slots)


def load_grads(here, g_refs, g_all, sem):
    copies = []
    rows = g_refs[0][0].shape[0]
    for cs in range(2):
        for dx in range(NX):
            at = ((here + dx) % NX) * (2 * HD)
            dst = g_all.at[pl.ds(cs * rows, rows), pl.ds(pl.multiple_of(at, 2 * HD), 2 * HD)]
            copies.append(pltpu.make_async_copy(g_refs[cs][dx], dst, sem.at[cs * NX + dx]))
            copies[-1].start()
    return copies


def input_kernel(here_ref, *rest):
    here = here_ref[0]
    g_refs = (rest[0:4], rest[4:8])
    w_refs, outs = rest[8:12], rest[12:20]
    g_all, w_all, result, sem, sem_w = rest[20:]
    copies = load_grads(here, g_refs, g_all, sem)
    for n in range(8):
        at = ((here + n // 2) % NX) * (2 * HD) + (n % 2) * HD
        dst = w_all.at[:, pl.ds(pl.multiple_of(at, HD), HD)]
        copies.append(pltpu.make_async_copy(w_refs[n // 2].at[n % 2], dst, sem_w.at[n]))
        copies[-1].start()
    for c in copies:
        c.wait()
    cols = w_all.shape[0]
    for at in range(0, cols, 2 * HD):
        c = pl.ds(at, min(2 * HD, cols - at))
        block = lax.dot_general(
            g_all[...], w_all[c, :], (((1,), (1,)), ((), ())), preferred_element_type=F32
        ).astype(BF)
        result[:, c] = block
    for n, out in enumerate(outs):
        row = (n // NX) * (NX * HD) + ((here + n) % NX) * HD
        out[...] = result[pl.ds(pl.multiple_of(row, HD), HD), :]


def input_blocks(here, g_slots, w_slots):
    cols = w_slots[0].shape[1]
    return pl.pallas_call(
        input_kernel,
        out_shape=tuple(jax.ShapeDtypeStruct((HD, cols), BF) for _ in range(8)),
        in_specs=[SM] + [HB] * 12,
        out_specs=(VM,) * 8,
        scratch_shapes=[
            pltpu.VMEM((8 * HD, 8 * HD), BF),
            pltpu.VMEM((cols, 8 * HD), BF),
            pltpu.VMEM((8 * HD, cols), BF),
            pltpu.SemaphoreType.DMA((8,)),
            pltpu.SemaphoreType.DMA((8,)),
        ],
        compiler_params=pltpu.CompilerParams(vmem_limit_bytes=BIG),
        cost_estimate=pl.CostEstimate(
            flops=2 * 1024 * 1024 * cols, bytes_accessed=7 * 1024 * 1024, transcendentals=0
        ),
        name="input_blocks",
    )(here, *g_slots[0], *g_slots[1], *w_slots)


def proj_kernel(x_ref, g0, g1, out, x_all, g_all, total, sem_x, sem_g, sem_out):
    rows = g0.shape[0]
    pieces, part = out.shape[0], out.shape[1]
    chunk = x_all.shape[0] // 4
    loads = []
    for n, g in enumerate((g0, g1)):
        loads.append(pltpu.make_async_copy(g, g_all.at[pl.ds(n * rows, rows), :], sem_g.at[n]))
        loads[-1].start()
    x_loads = []
    for j in range(4):
        r = pl.ds(j * chunk, chunk)
        for n in range(8):
            src = x_ref.at[n % NX, n // NX, r, :]
            dst = x_all.at[r, pl.ds(n * HD, HD)]
            x_loads.append(pltpu.make_async_copy(src, dst, sem_x.at[j * 8 + n]))
            x_loads[-1].start()
    for c in loads:
        c.wait()
    stores = []
    for j in range(4):
        for c in x_loads[j * 8 : j * 8 + 8]:
            c.wait()
        halves = [pl.ds(j * chunk + n * (chunk // 2), chunk // 2) for n in range(2)]
        sums = [jnp.dot(x_all[h, :], g_all[...], preferred_element_type=F32) for h in halves]
        for h, part_sum in zip(halves, sums):
            total[h, :] = part_sum.astype(BF)
        for n in range(j * pieces // 4, (j + 1) * pieces // 4):
            src = total.at[pl.ds(n * part, part), :]
            stores.append(pltpu.make_async_copy(src, out.at[n], sem_out.at[n]))
            stores[-1].start()
    for c in stores:
        c.wait()


def proj_parts(x_turned, g0, g1):
    cols = x_turned.shape[2]
    return pl.pallas_call(
        proj_kernel,
        out_shape=jax.ShapeDtypeStruct((16, cols // 16, 2 * HD), BF),
        in_specs=[HB] * 3,
        out_specs=HB,
        scratch_shapes=[
            pltpu.VMEM((cols, 8 * HD), BF),
            pltpu.VMEM((8 * HD, 2 * HD), BF),
            pltpu.VMEM((cols, 2 * HD), BF),
            pltpu.SemaphoreType.DMA((32,)),
            pltpu.SemaphoreType.DMA((2,)),
            pltpu.SemaphoreType.DMA((16,)),
        ],
        compiler_params=pltpu.CompilerParams(vmem_limit_bytes=BIG),
        cost_estimate=pl.CostEstimate(
            flops=2 * 1024 * 256 * cols, bytes_accessed=13 * 1024 * 1024, transcendentals=0
        ),
        name="proj_parts",
    )(x_turned, g0, g1)


def place_kernel(where_ref, *rest):
    core, here = where_ref[0], where_ref[1]
    parts, out = rest[:8], rest[8]
    cols = parts[0].shape[1]
    for cs in range(2):
        for dx in range(NX):
            at = ((core + cs) % 2) * (NX * cols) + ((here - dx + NX) % NX) * cols
            out[:, pl.ds(pl.multiple_of(at, HD), cols)] = parts[cs * NX + dx][...]


def place(where, parts):
    rows, cols = parts[0].shape
    return pl.pallas_call(
        place_kernel,
        out_shape=jax.ShapeDtypeStruct((rows, 8 * cols), BF),
        in_specs=[SM] + [VM] * 8,
        out_specs=VM,
        compiler_params=pltpu.CompilerParams(vmem_limit_bytes=BIG),
        name="place_columns",
    )(where, *parts)


def summed(*terms):
    total = terms[0].astype(F32)
    for term in terms[1:]:
        total = total + term.astype(F32)
    return total


def per_device(
    normed_input,
    queries,
    key_heads,
    value_heads,
    attn_out,
    out_grad,
    key_weight,
    value_weight,
    block_order,
):
    ctx = lax.axis_index("ctx")
    here = lax.axis_index("tensor")
    zh, y, core = ctx >> 3, (ctx >> 1) & 3, ctx & 1
    pp = lax.ppermute
    barrier = lax.optimization_barrier
    q_own, do_own, o_own = queries[0], out_grad[0], attn_out[0]

    half_cols = NH * HD

    def theirs(a):
        return lax.dynamic_slice_in_dim(a, (1 - core) * half_cols, half_cols, axis=1)

    def to_each(a, n):
        return jnp.broadcast_to(a[None], (n,) + a.shape).reshape(n * a.shape[0], a.shape[1])

    def exchange(a, axes, groups=None):
        return lax.all_to_all(a, axes, 0, 0, axis_index_groups=groups, tiled=True)

    k_out, q_first, v_own = barrier((to_each(key_heads[0].T, 8), q_own, value_heads[0]))
    q_got = pp(theirs(q_first), "ctx", CORE_PERM)
    k_mine = exchange(k_out, "ctx", CHIP_GROUPS)
    v_all = lax.all_gather(v_own.T, "ctx", axis=0, tiled=True)
    q_got, do_own, o_own, x_own, key_weight, value_weight = barrier(
        (q_got, do_own, o_own, normed_input[0], key_weight, value_weight)
    )
    do_o_got = pp(jnp.stack([theirs(do_own), theirs(o_own)]), "ctx", CORE_PERM)

    blocks = jnp.arange(block_order.shape[0], dtype=jnp.int32)
    owner = blocks >> 1
    k_slot = ((((owner & 1) ^ core) * 8) + (owner >> 1)) * 2 + (blocks & 1)
    v_slot = blocks
    to_slot = k_slot
    slots = jnp.concatenate([k_slot, v_slot, to_slot]).reshape(3, 1, -1)
    places = jnp.sum(jnp.where(slots == blocks[:, None], block_order, 0), axis=2)
    mine = jnp.stack([2 * ctx, 2 * ctx + 1, 2 * (ctx ^ 1), 2 * (ctx ^ 1) + 1])
    rank = jnp.sum(jnp.where(blocks[None, :] == mine[:, None], block_order[None, :], 0), axis=1)
    core1, here1 = core.reshape(1), here.reshape(1)

    cols = normed_input.shape[2] // 8
    x_halves = x_own.T.reshape(16, 2, -1, x_own.shape[0])

    def x_half(c):
        return lax.dynamic_index_in_dim(x_halves, c, 1, keepdims=False).reshape(NX * cols, -1)

    x_chip = jnp.stack([x_half(core), pp(x_half(1 - core), "ctx", CORE_PERM)])
    w_near = []
    for dx in range(NX):
        at = (core * NX + ((here - dx) & 3)) * cols
        w_near.append(
            jnp.stack([lax.dynamic_slice_in_dim(w, at, cols, axis=0) for w in (key_weight, value_weight)])
        )
    w_slots = w_near[:1] + [pp(w_near[d], "tensor", x_perm(-d)) for d in range(1, NX)]
    qaug, doaug, qT, doT = turned(core1, q_own, q_got, do_own, o_own, do_o_got)
    k_mine, qaug, x_chip = barrier((k_mine, qaug, x_chip))
    x_all = lax.all_gather(x_chip, "tensor")
    k_slots = [k_mine, pp(k_mine, "ctx", CORE_PERM)]
    lse = softmax_stats(rank, places[0], qaug, k_slots)
    lse, w_slots = barrier((lse, w_slots))
    v_slots = [v_all]
    dq_keep, dq_send, dkv0, dkv1 = attention_grads(
        rank, places, lse, qaug, doaug, qT, doT, k_slots, v_slots
    )

    chip = summed(dkv0, pp(dkv1, "ctx", CORE_PERM)).astype(BF)
    terms = lax.all_to_all(chip, "ctx", 0, 0, axis_index_groups=CHIP_GROUPS, tiled=True)
    grads = jnp.sum(terms.astype(F32), axis=0).astype(BF).T

    dq_got = pp(dq_send, "ctx", CORE_PERM)
    query_grad = jnp.where(
        core == 0,
        jnp.concatenate([dq_keep, dq_got], axis=1),
        jnp.concatenate([dq_got, dq_keep], axis=1),
    )

    grads, query_grad = barrier((grads, query_grad))
    g_own = [grads] + [pp(grads, "tensor", x_perm(-dx)) for dx in range(1, NX)]
    g_other = pp(grads, "ctx", CORE_PERM)
    pieces = proj_parts(x_all, grads, g_other)
    pieces, g_own = barrier((pieces, g_own))
    g_slots = (g_own, [g_other] + [pp(g, "ctx", CORE_PERM) for g in g_own[1:]])
    pieces = lax.all_to_all(
        pieces, ("dp", "ctx"), 0, 0, axis_index_groups=ALL_CHIP_GROUPS, tiled=True
    )
    outs = input_blocks(here1, g_slots, w_slots)
    got = [
        outs[n] if n == 0 else pp(outs[n], ("ctx", "tensor"), cx_perm(n // NX, n % NX))
        for n in range(8)
    ]
    input_grad = place(jnp.stack([core, here]), got)
    pieces, input_grad = barrier((pieces, input_grad))
    proj = jnp.sum(pieces.astype(F32), axis=0).astype(BF)
    return (query_grad[None], input_grad[None], proj[:, :HD], proj[:, HD:])


def solution(mesh):
    in_specs = (
        P("dp", ("ctx", "tensor"), None),
        P("dp", "ctx", "tensor"),
        P("dp", "ctx", "tensor"),
        P("dp", "ctx", "tensor"),
        P("dp", "ctx", "tensor"),
        P("dp", "ctx", "tensor"),
        P(None, "tensor"),
        P(None, "tensor"),
        P(),
    )
    out_specs = (
        P("dp", "ctx", "tensor"),
        P("dp", ("ctx", "tensor"), None),
        P(("dp", "ctx"), "tensor"),
        P(("dp", "ctx"), "tensor"),
    )
    return jax.shard_map(
        per_device, mesh=mesh, in_specs=in_specs, out_specs=out_specs, check_vma=False
    )
```
